1024 devices in a mesh: dp: 128 (over z, y, x_hi), tensor: 8 (over x_lo, core).
Axes of the slice: x: 8 (x_hi: 2, x_lo: 4; x = x_hi * 4 + x_lo), y: 8, z: 8, core: 2. Of those that a mesh axis runs over, the one named last changes fastest.
Arguments:
- queries: bfloat16 [512, 96, 8192], P('dp', None, 'tensor'), may hold values from -6 to 6
- keys: bfloat16 [512, 96, 1024], P('dp', None, 'tensor'), may hold values from -6 to 6
- values: bfloat16 [512, 96, 1024], P('dp', None, 'tensor'), may hold values from -6 to 6
- hidden: bfloat16 [512, 96, 5120], P('dp', None, 'tensor'), may hold values from -6 to 6
- grad_out: bfloat16 [512, 96, 8192], P('dp', None, 'tensor'), may hold values from -6 to 6
- group_alive: int32 [256], replicated, may hold values from 0 to 1, as said below
- positions: int32 [512, 96], P('dp'), may hold values from -47 to 95, as said below
Outputs:
- grad_queries: bfloat16 [512, 96, 8192], P('dp', None, 'tensor')
- grad_keys: bfloat16 [512, 96, 1024], P('dp', None, 'tensor')
- grad_weight: float32 [1024, 5120], P('dp', 'tensor')
The draws below stay inside these ranges and needn't reach their ends.
Inputs may be any that keep to these rules, and one draw needn't show every extreme that they name: `group_alive`: index i and index i + 64 of dp form a pair holding 2 * 2 rollout groups; in each pair exactly one of them has 0. Along a row the positions rise by one from a start of 0 or below.
All inputs are finite; a program needn't handle non-finite values.
Results may differ from the reference program's by a relative error of at most 0.0064.
Values may be sent and summed in bfloat16 or wider, within the bound.
A program may use at most 32 MiB of HBM per device.

```python
import jax
import jax.numpy as jnp
from jax import lax

D = 5120
HQ = 64
KVH = 8
HD = 128
L = 96
S_DEV = 4
GROUP = 2
ROWS = 512
N_DP = 128


def draw_group_alive(key, part):
    key = jax.random.fold_in(key, 11)
    half = N_DP // 2
    per_device = S_DEV // GROUP
    per_pair = 2 * per_device
    killed = jax.random.randint(key, (half,), 0, per_pair)
    group_ids = jnp.arange(per_pair)
    alive = jnp.where(group_ids[None, :] == killed[:, None], 0, 1).astype(jnp.int32)
    return jnp.concatenate([alive[:, :per_device].reshape(-1), alive[:, per_device:].reshape(-1)], axis=0)


def draw_positions(key, part):
    key = jax.random.fold_in(key, 3)
    padding = jax.random.randint(key, (ROWS,), 0, L // 2)
    return (jnp.arange(L)[None, :] - padding[:, None]).astype(jnp.int32)


def draw_queries(key, part):
    fresh = jax.random.fold_in(key, 5)
    drawn = jnp.clip(jax.random.normal(fresh, (ROWS, L, KVH, HQ // KVH, HD), jnp.float32), -6.0, 6.0)
    return drawn.reshape(ROWS, L, HQ * HD).astype(jnp.bfloat16)


def draw_keys(key, part):
    fresh = jax.random.fold_in(key, 6)
    drawn = jnp.clip(jax.random.normal(fresh, (ROWS, L, KVH, HD), jnp.float32), -6.0, 6.0)
    return drawn.reshape(ROWS, L, KVH * HD).astype(jnp.bfloat16)


def block_scale(stream_key, shape, pieces, low, high):
    level = 1.0
    for position, parts in pieces:
        heights = jax.random.uniform(jax.random.fold_in(jax.random.fold_in(stream_key, 6), position), (parts,), jnp.float32, low / len(pieces), high / len(pieces))
        level = level * jnp.repeat(jnp.exp(heights), shape[position] // parts).reshape((-1,) + (1,) * (len(shape) - 1 - position))
    return level


def bell_draw(own_key, dims, spread, limit, shards=(), kind=jnp.bfloat16):
    gain = block_scale(own_key, dims, shards, -0.22, 0.18) if shards else 1.0
    result = jax.random.normal(own_key, dims, jnp.float32) * spread * gain
    return jnp.minimum(jnp.maximum(result, -limit), limit).astype(kind)


def setup_inputs(seed: int = 0) -> dict:
    arg_keys = jax.random.split(jax.random.key(seed), 8)
    return {
        "queries": draw_queries(jax.random.fold_in(arg_keys[7], 71), 0),
        "keys": draw_keys(jax.random.fold_in(arg_keys[7], 71), 0),
        "values": bell_draw(arg_keys[2], (ROWS, L, KVH * HD), 1.0, 6.0, ((0, 128), (2, 8))),
        "hidden": bell_draw(arg_keys[3], (ROWS, L, D), 1.0, 6.0, ((0, 128), (2, 8))),
        "grad_out": bell_draw(arg_keys[4], (ROWS, L, HQ * HD), 1.0, 6.0, ((0, 128), (2, 8))),
        "group_alive": draw_group_alive(jax.random.fold_in(arg_keys[7], 71), 0),
        "positions": draw_positions(jax.random.fold_in(arg_keys[7], 71), 0),
    }


def round_half(array):
    return lax.optimization_barrier(array.astype(jnp.bfloat16)).astype(jnp.float32)


def attend(query_rows, key_rows, value_rows, grad_rows, key_valid):
    length = query_rows.shape[0]
    kv_heads = key_rows.shape[-1] // HD
    q_group = query_rows.shape[-1] // HD // kv_heads
    query_f = query_rows.astype(jnp.float32).reshape(length, kv_heads, q_group, HD)
    key_f = key_rows.astype(jnp.float32).reshape(length, kv_heads, HD)
    value_f = value_rows.astype(jnp.float32).reshape(length, kv_heads, HD)
    grad_f = grad_rows.astype(jnp.float32).reshape(length, kv_heads, q_group, HD)
    factor = HD ** -0.5
    scores = jnp.einsum("qhgd,khd->hgqk", query_f, key_f) * factor
    q_index = jnp.arange(length)[:, None]
    k_index = jnp.arange(length)[None, :]
    allowed = (k_index <= q_index) & ((key_valid[None, :] > 0) | (k_index == q_index))
    scores = jnp.where(allowed, scores, jnp.float32(-1e30))
    top_score = jnp.max(scores, axis=-1, keepdims=True)
    expo = jnp.exp(scores - top_score)
    probs = expo / jnp.sum(expo, axis=-1, keepdims=True)
    probs_half = round_half(probs)
    attended = jnp.einsum("hgqk,khd->qhgd", probs_half, value_f)
    delta = jnp.transpose(jnp.sum(grad_f * attended, axis=-1), (1, 2, 0))
    dprobs = jnp.einsum("qhgd,khd->hgqk", grad_f, value_f)
    dscores = probs * (dprobs - delta[..., None])
    dscores_half = round_half(dscores)
    grad_query = jnp.einsum("hgqk,khd->qhgd", dscores_half, key_f) * factor
    grad_key = jnp.einsum("hgqk,qhgd->khd", dscores_half, query_f) * factor
    grad_value = jnp.einsum("hgqk,qhgd->khd", probs_half, grad_f)
    return grad_query.reshape(length, -1), grad_key.reshape(length, -1), grad_value.reshape(length, -1)


def reference(queries, keys, values, hidden, grad_out, group_alive, positions):
    alive_row = jnp.repeat(group_alive, GROUP)
    masked = grad_out * alive_row.astype(grad_out.dtype)[:, None, None]
    key_valid = (positions >= 0).astype(jnp.float32)

    def one_row(packed):
        return attend(*packed)

    grad_query, grad_key, grad_value = lax.map(one_row, (queries, keys, values, masked, key_valid))
    grad_value = grad_value.astype(jnp.bfloat16)
    total_rows = grad_value.shape[0] * grad_value.shape[1]
    grad_weight = lax.dot_general(grad_value.reshape(total_rows, -1), hidden.reshape(total_rows, -1), (((0,), (0,)), ((), ())), preferred_element_type=jnp.float32)
    return grad_query.astype(jnp.bfloat16), grad_key.astype(jnp.bfloat16), grad_weight
```

```python
import jax
import jax.numpy as jnp
from jax import lax
from jax.experimental import pallas as pl
from jax.experimental.pallas import tpu as pltpu
from jax.sharding import PartitionSpec as P

HD = 128
GROUP = 2
N = 8
MESH = pl.DeviceIdType.MESH
F32 = jnp.float32
BF16 = jnp.bfloat16


def contract(a, b, dims):
    return lax.dot_general(a, b, ((dims[:1], dims[1:]), ((), ())), preferred_element_type=F32)


def heads_to_rows(x):
    return jnp.concatenate([x[:, h * HD : (h + 1) * HD] for h in range(x.shape[1] // HD)], axis=0)


def kernel(
    alive_ref, pos_ref, q_hbm, k_hbm, v_hbm, h_hbm, g_hbm,
    dq_hbm, dk_hbm, gw_ref,
    q_buf, k_buf, v_buf, g_buf, h_buf, mask_buf, p_buf, gv_buf, dq_buf, dk_buf,
    gv_send, gv_recv, gv_chunk, part, r_send, r_recv, s2_send, s2_recv, s3_send, s3_recv,
    in_sem, h_sem, out_sem, gs_sem, gr_sem, rs_sem, rr_sem, s2s_sem, s2r_sem, s3s_sem, s3r_sem,
):
    rows, length, _ = q_buf.shape
    cols = h_buf.shape[-1]
    heads = q_buf.shape[-1] // HD
    width = heads * length
    factor = HD**-0.5

    dp = lax.axis_index("dp")
    tensor = lax.axis_index("tensor")
    core = lax.rem(tensor, 2)
    x_hi = lax.rem(dp, 2)
    y = lax.rem(dp // 2, N)
    z = dp // (2 * N)
    stride = 2 * N - (2 * N - 2) * core
    ring = z * (1 - core) + y * core
    stride2 = 2 + (2 * N - 2) * core
    ring2 = y * (1 - core) + z * core

    def on_ring(d):
        return dp + (lax.rem(ring + d + N, N) - ring) * stride

    def on_ring2(d):
        return dp + (lax.rem(ring2 + d, N) - ring2) * stride2

    peers = [(dp, lax.rem(tensor + d, N)) for d in range(1, N)]
    peers += [(on_ring(1), tensor), (on_ring(-1), tensor)]
    peers += [(on_ring2(d), tensor) for d in range(1, N)]
    far = dp + 1 - 2 * x_hi
    peers += [(far, tensor), (far, tensor + 1 - 2 * core)]

    barrier = pltpu.get_barrier_semaphore()
    for peer in peers:
        pl.semaphore_signal(barrier, inc=1, device_id=peer, device_id_type=MESH)

    def load_row(r):
        return (
            pltpu.make_async_copy(q_hbm.at[r], q_buf.at[r], in_sem.at[r]),
            pltpu.make_async_copy(g_hbm.at[r], g_buf.at[r], in_sem.at[rows + r]),
        )

    load_k = pltpu.make_async_copy(k_hbm, k_buf, in_sem.at[2 * rows])
    load_v = pltpu.make_async_copy(v_hbm, v_buf, in_sem.at[2 * rows + 1])
    load_h = pltpu.make_async_copy(h_hbm, h_buf.at[core], in_sem.at[2 * rows + 2])
    load_k.start()
    for r in range(rows):
        for copy in load_row(r):
            copy.start()
    load_v.start()
    load_h.start()

    k_index = lax.broadcasted_iota(jnp.int32, (length, width), 0)
    lane = lax.broadcasted_iota(jnp.int32, (length, width), 1)
    q_index = lane
    for h in range(1, heads):
        q_index = jnp.where(lane >= h * length, lane - h * length, q_index)
    mask_buf[...] = jnp.where(k_index < q_index, k_index, jnp.where(k_index == q_index, length, -1))

    def masked_grad(r):
        alive = alive_ref[dp * (rows // GROUP) + r // GROUP].astype(F32).astype(BF16)
        return heads_to_rows(g_buf[r] * alive)

    load_k.wait()

    def forward(r, carry):
        for copy in load_row(r):
            copy.wait()
        queries = heads_to_rows(q_buf[r])
        grads = masked_grad(r)
        scores = contract(k_buf[r], queries, (1, 1)) * factor
        scores = jnp.where(mask_buf[...] >= -pos_ref[r, 0], scores, F32(-1e30))
        expo = jnp.exp(scores - jnp.max(scores, axis=0, keepdims=True))
        probs = expo * (1.0 / jnp.sum(expo, axis=0, keepdims=True))
        p_buf[r] = probs
        at = pl.ds(pl.multiple_of(r * length, length), length)
        gv_buf[at, :] = contract(probs.astype(BF16), grads, (1, 0))
        return carry

    lax.fori_loop(0, rows, forward, 0)

    value_grad = gv_buf[...].T
    tokens = value_grad.shape[1]
    value_grad = value_grad.reshape(HD // 16, 2, 8, tokens)
    for c in range(2):
        gv_send[c] = value_grad[:, c].reshape(HD // 2, tokens).astype(BF16)

    pl.semaphore_wait(barrier, len(peers))

    def give(d):
        to = lax.rem(tensor + d, N)
        return pltpu.make_async_remote_copy(
            src_ref=gv_send.at[lax.rem(to, 2)], dst_ref=gv_recv.at[tensor],
            send_sem=gs_sem.at[d], recv_sem=gr_sem.at[tensor],
            device_id=(dp, to), device_id_type=MESH,
        )

    def take(d):
        of = lax.rem(tensor + d, N)
        return pltpu.make_async_remote_copy(
            src_ref=gv_send.at[0], dst_ref=gv_recv.at[of],
            send_sem=gs_sem.at[d], recv_sem=gr_sem.at[of],
            device_id=(dp, of), device_id_type=MESH,
        )

    for d in (4, 3, 5, 2, 6, 1, 7):
        give(d).start()
    swap_h = pltpu.make_async_remote_copy(
        src_ref=h_hbm, dst_ref=h_buf.at[core], send_sem=h_sem.at[0], recv_sem=h_sem.at[1],
        device_id=(dp, tensor + 1 - 2 * core), device_id_type=MESH,
    )
    swap_h.start()
    gv_recv[tensor] = gv_send[core]
    load_v.wait()

    def store_row(r):
        return pltpu.make_async_copy(dq_buf.at[r], dq_hbm.at[r], out_sem.at[r])

    def backward(r, carry):
        queries = heads_to_rows(q_buf[r])
        grads = masked_grad(r)
        probs = p_buf[r]
        dprobs = contract(v_buf[r], grads, (1, 1))
        delta = jnp.sum(probs.astype(BF16).astype(F32) * dprobs, axis=0, keepdims=True)
        dscores = (probs * (dprobs - delta)).astype(BF16)
        dk_buf[r] = (contract(dscores, queries, (1, 0)) * factor).astype(BF16)
        dq = (contract(dscores, k_buf[r], (0, 0)) * factor).astype(BF16)
        for h in range(heads):
            dq_buf[r, :, h * HD : (h + 1) * HD] = dq[h * length : (h + 1) * length]
        store_row(r).start()
        return carry

    lax.fori_loop(0, rows, backward, 0)
    store_dk = pltpu.make_async_copy(dk_buf, dk_hbm, out_sem.at[rows])
    store_dk.start()

    for d in (1, 7, 2, 6, 3, 5, 4):
        take(d).wait_recv()

    @pl.when(core == 0)
    def _():
        gv_chunk[...] = gv_recv[...]

    @pl.when(core == 1)
    def _():
        for t in range(N):
            gv_chunk[t] = jnp.concatenate(
                [gv_recv[h].astype(F32)[8 * t : 8 * t + 8] for h in range(N)], axis=0
            ).astype(BF16)

    load_h.wait()
    swap_h.wait_recv()

    def product(d, k):
        at = lax.rem(ring + d + N, N)
        hidden = h_buf[k].reshape(tokens, cols)
        return contract(gv_chunk[at], hidden, (1, 0))

    def hop(way, k, j):
        return pltpu.make_async_remote_copy(
            src_ref=r_send.at[way, k, j], dst_ref=r_recv.at[way, k, j],
            send_sem=rs_sem.at[way, k, j], recv_sem=rr_sem.at[way, k, j],
            device_id=(on_ring(1 - 2 * way), tensor), device_id_type=MESH,
        )

    def ahead(way, j):
        return (4 - j) * (1 - 2 * way)

    for way, k, j in ((0, 0, 0), (1, 1, 0), (0, 1, 1), (1, 0, 1)):
        r_send[way, k, j] = product(ahead(way, j), k).astype(BF16)
        hop(way, k, j).start()
    for j in range(1, 4):
        for first in (True, False):
            pair = ((0, 0), (1, 1)) if first else ((0, 1), (1, 0))
            step = j if first else j + 1
            if step == 4:
                continue
            for way, k in pair:
                part[way] = product(ahead(way, step), k)
            for way, k in pair:
                hop(way, k, step - 1).wait_recv()
                r_send[way, k, step] = (part[way] + r_recv[way, k, step - 1].astype(F32)).astype(BF16)
                hop(way, k, step).start()
    for k in range(2):
        part[k] = product(0, k)
    sums = []
    for k in range(2):
        total = part[k]
        for way in range(2):
            hop(way, k, 3).wait_recv()
            total = total + r_recv[way, k, 3].astype(F32)
        sums.append(total.reshape(N, 8, cols))
    s2_send[...] = jnp.concatenate(sums, axis=1).astype(BF16)

    def cross(d):
        to = lax.rem(ring2 + d, N)
        return pltpu.make_async_remote_copy(
            src_ref=s2_send.at[to], dst_ref=s2_recv.at[ring2],
            send_sem=s2s_sem.at[d], recv_sem=s2r_sem.at[ring2],
            device_id=(on_ring2(d), tensor), device_id_type=MESH,
        )

    def cross_in(d):
        of = lax.rem(ring2 + d, N)
        return pltpu.make_async_remote_copy(
            src_ref=s2_send.at[of], dst_ref=s2_recv.at[of],
            send_sem=s2s_sem.at[d], recv_sem=s2r_sem.at[of],
            device_id=(on_ring2(d), tensor), device_id_type=MESH,
        )

    for d in (4, 3, 5, 2, 6, 1, 7):
        cross(d).start()
    total = s2_send[ring2].astype(F32)
    for d in (1, 7, 2, 6, 3, 5, 4):
        cross_in(d).wait_recv()
        total = total + s2_recv[lax.rem(ring2 + d, N)].astype(F32)
    for k in range(2):
        s3_send[k] = total[8 * k : 8 * k + 8]

    def finish(k):
        return pltpu.make_async_remote_copy(
            src_ref=s3_send.at[k], dst_ref=s3_recv.at[x_hi],
            send_sem=s3s_sem.at[k], recv_sem=s3r_sem.at[x_hi],
            device_id=(dp - x_hi + core, tensor - core + k), device_id_type=MESH,
        )

    def finish_in(of):
        return pltpu.make_async_remote_copy(
            src_ref=s3_send.at[0], dst_ref=s3_recv.at[of],
            send_sem=s3s_sem.at[0], recv_sem=s3r_sem.at[of],
            device_id=(far, tensor), device_id_type=MESH,
        )

    home = x_hi == core

    @pl.when(home)
    def _():
        finish(1 - core).start()
        finish_in(1 - x_hi).wait_recv()
        gw_ref[...] = s3_send[core] + s3_recv[1 - x_hi]
        finish(1 - core).wait_send()

    @pl.when(jnp.logical_not(home))
    def _():
        for k in range(2):
            finish(k).start()
        for of in range(2):
            finish_in(of).wait_recv()
        gw_ref[...] = s3_recv[0] + s3_recv[1]
        for k in range(2):
            finish(k).wait_send()

    for d in range(1, N):
        give(d).wait_send()
        cross(d).wait_send()
    swap_h.wait_send()
    for way in range(2):
        for k in range(2):
            for j in range(0 if way == k else 1, 4):
                hop(way, k, j).wait_send()
    for r in range(rows):
        store_row(r).wait()
    store_dk.wait()


def local(queries, keys, values, hidden, grad_out, group_alive, positions):
    rows, length, model = queries.shape
    cols = hidden.shape[-1]
    heads = model // HD
    width = heads * length
    tokens = rows * length
    half = HD // 2
    anywhere = pl.BlockSpec(memory_space=pl.ANY)
    scalar = pl.BlockSpec(memory_space=pltpu.SMEM)
    dma = pltpu.SemaphoreType.DMA
    return pl.pallas_call(
        kernel,
        out_shape=(
            jax.ShapeDtypeStruct(queries.shape, BF16),
            jax.ShapeDtypeStruct(keys.shape, BF16),
            jax.ShapeDtypeStruct((8, cols), F32),
        ),
        in_specs=[scalar, scalar] + [anywhere] * 5,
        out_specs=(anywhere, anywhere, pl.BlockSpec(memory_space=pltpu.VMEM)),
        scratch_shapes=[
            pltpu.VMEM(queries.shape, BF16),
            pltpu.VMEM(keys.shape, BF16),
            pltpu.VMEM(keys.shape, BF16),
            pltpu.VMEM(queries.shape, BF16),
            pltpu.VMEM((2,) + hidden.shape, BF16),
            pltpu.VMEM((length, width), jnp.int32),
            pltpu.VMEM((rows, length, width), F32),
            pltpu.VMEM((tokens, HD), F32),
            pltpu.VMEM(queries.shape, BF16),
            pltpu.VMEM(keys.shape, BF16),
            pltpu.VMEM((2, half, tokens), BF16),
            pltpu.VMEM((N, half, tokens), BF16),
            pltpu.VMEM((N, half, tokens), BF16),
            pltpu.VMEM((2, half, cols), F32),
            pltpu.VMEM((2, 2, 4, half, cols), BF16),
            pltpu.VMEM((2, 2, 4, half, cols), BF16),
            pltpu.VMEM((N, 16, cols), BF16),
            pltpu.VMEM((N, 16, cols), BF16),
            pltpu.VMEM((2, 8, cols), F32),
            pltpu.VMEM((2, 8, cols), F32),
            dma((2 * rows + 3,)),
            dma((2,)),
            dma((rows + 1,)),
            dma((N,)),
            dma((N,)),
            dma((2, 2, 4)),
            dma((2, 2, 4)),
            dma((N,)),
            dma((N,)),
            dma((2,)),
            dma((2,)),
        ],
        compiler_params=pltpu.CompilerParams(
            collective_id=0, has_side_effects=True, vmem_limit_bytes=40 * 1024 * 1024
        ),
        cost_estimate=pl.CostEstimate(
            flops=10 * width * length * HD * rows + 2 * tokens * 1024 * cols,
            bytes_accessed=4000000,
            transcendentals=rows * width * length,
        ),
    )(group_alive, positions, queries, keys, values, hidden, grad_out)


def solution(mesh):
    return jax.shard_map(
        local,
        mesh=mesh,
        in_specs=(
            P("dp", None, "tensor"),
            P("dp", None, "tensor"),
            P("dp", None, "tensor"),
            P("dp", None, "tensor"),
            P("dp", None, "tensor"),
            P(),
            P("dp", None),
        ),
        out_specs=(P("dp", None, "tensor"), P("dp", None, "tensor"), P("dp", "tensor")),
        check_vma=False,
    )
```

```python
import jax
import jax.numpy as jnp
from jax import lax
from jax.experimental import pallas as pl
from jax.experimental.pallas import tpu as pltpu
from jax.sharding import PartitionSpec as P

HD = 128
GROUP = 2
N = 8
MESH = pl.DeviceIdType.MESH
F32 = jnp.float32
BF16 = jnp.bfloat16


def contract(a, b, dims):
    return lax.dot_general(a, b, ((dims[:1], dims[1:]), ((), ())), preferred_element_type=F32)


def heads_to_rows(x):
    return jnp.concatenate([x[:, h * HD : (h + 1) * HD] for h in range(x.shape[1] // HD)], axis=0)


def kernel(
    q_hbm, k_hbm, v_hbm, h_hbm, g_hbm, alive_hbm, pos_hbm,
    dq_ref, dk_ref, gw_ref,
    q_buf, k_buf, v_buf, g_buf, h_buf, mask_buf, p_buf, gv_buf, alive_ref, pos_ref,
    gv_half, gv_whole, gv_recv, gv_chunk, part, r_send, r_recv, s2_send, s2_recv, s3_send, s3_recv,
    in_sem, h_sem, gs_sem, gr_sem, ws_sem, wr_sem, rs_sem, rr_sem, s2s_sem, s2r_sem, s3s_sem, s3r_sem,
):
    rows, length, _ = q_buf.shape
    cols = h_buf.shape[-1]
    heads = q_buf.shape[-1] // HD
    width = heads * length
    tokens = rows * length
    factor = HD**-0.5
    piece = HD // 4

    dp = lax.axis_index("dp")
    tensor = lax.axis_index("tensor")
    core = lax.rem(tensor, 2)
    x_hi = lax.rem(dp, 2)
    y = lax.rem(dp // 2, N)
    z = dp // (2 * N)
    stride = 2 * N - (2 * N - 2) * core
    ring = z * (1 - core) + y * core
    stride2 = 2 + (2 * N - 2) * core
    ring2 = y * (1 - core) + z * core

    def on_ring(d):
        return dp + (lax.rem(ring + d + N, N) - ring) * stride

    def at_ring2(place):
        return dp + (place - ring2) * stride2

    load_scalars = (
        pltpu.make_async_copy(alive_hbm, alive_ref, in_sem.at[2 * rows + 3]),
        pltpu.make_async_copy(pos_hbm, pos_ref, in_sem.at[2 * rows + 4]),
    )

    def load_row(r):
        return (
            pltpu.make_async_copy(q_hbm.at[r], q_buf.at[r], in_sem.at[r]),
            pltpu.make_async_copy(g_hbm.at[r], g_buf.at[r], in_sem.at[rows + r]),
        )

    load_k = pltpu.make_async_copy(k_hbm, k_buf, in_sem.at[2 * rows])
    load_v = pltpu.make_async_copy(v_hbm, v_buf, in_sem.at[2 * rows + 1])
    load_h = pltpu.make_async_copy(h_hbm, h_buf.at[core], in_sem.at[2 * rows + 2])
    for copy in load_scalars:
        copy.start()
    load_k.start()
    for r in range(rows):
        for copy in load_row(r):
            copy.start()
    load_v.start()
    load_h.start()

    far = dp + 1 - 2 * x_hi
    peers = [(far, tensor), (far, tensor + 1 - 2 * core)]
    peers += [(at_ring2(lax.rem(ring2 + d, N)), tensor) for d in range(1, N)]
    peers += [(dp, lax.rem(tensor + d, N)) for d in range(1, N)]
    peers += [(on_ring(1), tensor), (on_ring(-1), tensor)]
    barrier = pltpu.get_barrier_semaphore()
    for peer in peers:
        pl.semaphore_signal(barrier, inc=1, device_id=peer, device_id_type=MESH)

    k_index = lax.broadcasted_iota(jnp.int32, (length, width), 0)
    lane = lax.broadcasted_iota(jnp.int32, (length, width), 1)
    q_index = lane
    for h in range(1, heads):
        q_index = jnp.where(lane >= h * length, lane - h * length, q_index)
    mask_buf[...] = jnp.where(k_index < q_index, k_index, jnp.where(k_index == q_index, length, -1))

    def masked_grad(r):
        alive = alive_ref[dp * (rows // GROUP) + r // GROUP].astype(F32).astype(BF16)
        return heads_to_rows(g_buf[r] * alive)

    for copy in load_scalars:
        copy.wait()
    load_k.wait()

    def forward(r, carry):
        for copy in load_row(r):
            copy.wait()
        queries = heads_to_rows(q_buf[r])
        grads = masked_grad(r)
        scores = contract(k_buf[r], queries, (1, 1)) * factor
        scores = jnp.where(mask_buf[...] >= -pos_ref[r, 0], scores, F32(-1e30))
        expo = jnp.exp(scores - jnp.max(scores, axis=0, keepdims=True))
        probs = expo * (1.0 / jnp.sum(expo, axis=0, keepdims=True))
        p_buf[r] = probs
        at = pl.ds(pl.multiple_of(r * length, length), length)
        gv_buf[at, :] = contract(probs.astype(BF16), grads, (1, 0))
        return carry

    lax.fori_loop(0, rows, forward, 0)

    value_grad = gv_buf[...].T.reshape(HD // 16, 2, 8, tokens)
    for s in range(2):
        gv_half[s] = value_grad[4 * s : 4 * s + 4, 0].reshape(piece, tokens).astype(BF16)
    gv_whole[...] = value_grad[:, 1].reshape(2 * piece, tokens).astype(BF16)

    pl.semaphore_wait(barrier, len(peers))

    def give_half(s, chip):
        return pltpu.make_async_remote_copy(
            src_ref=gv_half.at[s], dst_ref=gv_chunk.at[s, tensor],
            send_sem=gs_sem.at[s, chip], recv_sem=gr_sem.at[s, tensor],
            device_id=(dp, 2 * chip), device_id_type=MESH,
        )

    def take_half(s, of):
        return pltpu.make_async_remote_copy(
            src_ref=gv_half.at[s], dst_ref=gv_chunk.at[s, of],
            send_sem=gs_sem.at[s, 0], recv_sem=gr_sem.at[s, of],
            device_id=(dp, of), device_id_type=MESH,
        )

    def give_whole(chip):
        return pltpu.make_async_remote_copy(
            src_ref=gv_whole, dst_ref=gv_recv.at[tensor],
            send_sem=ws_sem.at[chip], recv_sem=wr_sem.at[tensor],
            device_id=(dp, 2 * chip + 1), device_id_type=MESH,
        )

    def take_whole(of):
        return pltpu.make_async_remote_copy(
            src_ref=gv_whole, dst_ref=gv_recv.at[of],
            send_sem=ws_sem.at[0], recv_sem=wr_sem.at[of],
            device_id=(dp, of), device_id_type=MESH,
        )

    chips = N // 2
    own = tensor // 2
    away = [lax.rem(own + d, chips) for d in (2, 1, 3)]
    for s in range(2):
        for chip in away:
            give_half(s, chip).start()

        @pl.when(core == s)
        def _():
            for chip in away:
                give_whole(chip).start()

        @pl.when(core == 1)
        def _():
            give_half(s, own).start()

    @pl.when(core == 0)
    def _():
        give_whole(own).start()
        for s in range(2):
            gv_chunk[s, tensor] = gv_half[s]

    @pl.when(core == 1)
    def _():
        gv_recv[tensor] = gv_whole[...]

    swap_h = pltpu.make_async_remote_copy(
        src_ref=h_hbm, dst_ref=h_buf.at[core], send_sem=h_sem.at[0], recv_sem=h_sem.at[1],
        device_id=(dp, tensor + 1 - 2 * core), device_id_type=MESH,
    )
    swap_h.start()
    load_v.wait()

    def backward(r, carry):
        queries = heads_to_rows(q_buf[r])
        grads = masked_grad(r)
        probs = p_buf[r]
        dprobs = contract(v_buf[r], grads, (1, 1))
        delta = jnp.sum(probs.astype(BF16).astype(F32) * dprobs, axis=0, keepdims=True)
        dscores = (probs * (dprobs - delta)).astype(BF16)
        dk_ref[r] = (contract(dscores, queries, (1, 0)) * factor).astype(BF16)
        dq = (contract(dscores, k_buf[r], (0, 0)) * factor).astype(BF16)
        for h in range(heads):
            dq_ref[r, :, h * HD : (h + 1) * HD] = dq[h * length : (h + 1) * length]
        return carry

    lax.fori_loop(0, rows, backward, 0)
    load_h.wait()
    swap_h.wait_recv()

    def gathered(s):
        @pl.when(core == 0)
        def _():
            for d in range(1, N):
                take_half(s, lax.rem(tensor + d, N)).wait_recv()

        @pl.when(core == 1)
        def _():
            for chip in range(chips):
                of = 2 * chip + s

                @pl.when(of != tensor)
                def _():
                    take_whole(of).wait_recv()

            parts = [gv_recv[2 * chip + s].astype(F32) for chip in range(chips)]
            for t in range(N):
                gv_chunk[s, t] = jnp.concatenate([x[8 * t : 8 * t + 8] for x in parts], axis=0).astype(BF16)

    def products(s, offsets):
        left = jnp.concatenate([gv_chunk[s, lax.rem(ring + d + N, N)] for d in offsets], axis=0)
        for k in range(2):
            both = contract(left, h_buf[k].reshape(tokens, cols), (1, 0))
            for i in range(len(offsets)):
                part[s, i, k] = both[i * piece : (i + 1) * piece]

    def hop(way, s, j):
        return pltpu.make_async_remote_copy(
            src_ref=r_send.at[way, s, j], dst_ref=r_recv.at[way, s, j],
            send_sem=rs_sem.at[way, s, j], recv_sem=rr_sem.at[way, s, j],
            device_id=(on_ring(1 - 2 * way), tensor), device_id_type=MESH,
        )

    def first_sends(s):
        products(s, (4,))
        r_send[s, s, 0] = part[s, 0].astype(BF16)
        hop(s, s, 0).start()
        products(s, (3, -3))
        r_send[1 - s, s, 1] = part[s, 1 - s].astype(BF16)
        hop(1 - s, s, 1).start()

    def pass_on(way, s, j):
        hop(way, s, j - 1).wait_recv()
        r_send[way, s, j] = (part[s, way] + r_recv[way, s, j - 1].astype(F32)).astype(BF16)
        hop(way, s, j).start()

    def round_two(s):
        pass_on(s, s, 1)
        products(s, (2, -2))

    def round_three(s):
        for way in (1 - s, s):
            pass_on(way, s, 2)
        products(s, (1, -1))

    def round_four(s):
        for way in (1 - s, s):
            pass_on(way, s, 3)
        products(s, (0,))

    def place2(i):
        return i * (1 - core) + (2 * (i % 4) + i // 4) * core

    def cross(i):
        return pltpu.make_async_remote_copy(
            src_ref=s2_send.at[i], dst_ref=s2_recv.at[ring2],
            send_sem=s2s_sem.at[i], recv_sem=s2r_sem.at[ring2],
            device_id=(at_ring2(place2(i)), tensor), device_id_type=MESH,
        )

    def cross_in(of):
        return pltpu.make_async_remote_copy(
            src_ref=s2_send.at[0], dst_ref=s2_recv.at[of],
            send_sem=s2s_sem.at[0], recv_sem=s2r_sem.at[of],
            device_id=(at_ring2(of), tensor), device_id_type=MESH,
        )

    def if_away(i, act):
        @pl.when(place2(i) != ring2)
        def _():
            act(cross(i))

    def ring_end(s):
        total = part[s, 0]
        for way in (1 - s, s):
            hop(way, s, 3).wait_recv()
            total = total + r_recv[way, s, 3].astype(F32)
        total = total.reshape(2, 4, 8, cols)
        s2_send[4 * s : 4 * s + 4] = jnp.concatenate([total[0], total[1]], axis=1).astype(BF16)
        for i in range(4 * s, 4 * s + 4):
            if_away(i, lambda copy: copy.start())

    gathered(0)
    first_sends(0)
    round_two(0)
    gathered(1)
    first_sends(1)
    round_three(0)
    round_two(1)
    round_four(0)
    round_three(1)
    ring_end(0)
    round_four(1)
    ring_end(1)

    mine = ring2 * (1 - core) + (ring2 // 2 + 4 * lax.rem(ring2, 2)) * core
    total = s2_send[mine].astype(F32)
    for d in (1, 7, 2, 6, 3, 5, 4):
        of = lax.rem(ring2 + d, N)
        cross_in(of).wait_recv()
        total = total + s2_recv[of].astype(F32)
    for k in range(2):
        s3_send[k] = total[8 * k : 8 * k + 8]

    def finish(k):
        return pltpu.make_async_remote_copy(
            src_ref=s3_send.at[k], dst_ref=s3_recv.at[x_hi],
            send_sem=s3s_sem.at[k], recv_sem=s3r_sem.at[x_hi],
            device_id=(dp - x_hi + core, tensor - core + k), device_id_type=MESH,
        )

    def finish_in(of):
        return pltpu.make_async_remote_copy(
            src_ref=s3_send.at[0], dst_ref=s3_recv.at[of],
            send_sem=s3s_sem.at[0], recv_sem=s3r_sem.at[of],
            device_id=(far, tensor), device_id_type=MESH,
        )

    home = x_hi == core

    @pl.when(home)
    def _():
        finish(1 - core).start()

    @pl.when(jnp.logical_not(home))
    def _():
        for k in range(2):
            finish(k).start()

    for s in range(2):
        for chip in away:
            give_half(s, chip).wait_send()
        for way in range(2):
            for j in range(0 if way == s else 1, 4):
                hop(way, s, j).wait_send()
    for chip in away:
        give_whole(chip).wait_send()

    @pl.when(core == 0)
    def _():
        give_whole(own).wait_send()

    @pl.when(core == 1)
    def _():
        for s in range(2):
            give_half(s, own).wait_send()

    for i in range(N):
        if_away(i, lambda copy: copy.wait_send())
    swap_h.wait_send()

    @pl.when(home)
    def _():
        finish_in(1 - x_hi).wait_recv()
        gw_ref[...] = s3_send[core] + s3_recv[1 - x_hi]
        finish(1 - core).wait_send()

    @pl.when(jnp.logical_not(home))
    def _():
        for of in range(2):
            finish_in(of).wait_recv()
        gw_ref[...] = s3_recv[0] + s3_recv[1]
        for k in range(2):
            finish(k).wait_send()


def local(queries, keys, values, hidden, grad_out, group_alive, positions):
    rows, length, model = queries.shape
    cols = hidden.shape[-1]
    heads = model // HD
    width = heads * length
    tokens = rows * length
    piece = HD // 4
    anywhere = pl.BlockSpec(memory_space=pl.ANY)
    inside = pl.BlockSpec(memory_space=pltpu.VMEM)
    dma = pltpu.SemaphoreType.DMA
    inputs = (queries, keys, values, hidden, grad_out, group_alive, positions)
    return pl.pallas_call(
        kernel,
        out_shape=(
            pltpu.VMEM(queries.shape, BF16),
            pltpu.VMEM(keys.shape, BF16),
            pltpu.VMEM((8, cols), F32),
        ),
        in_specs=[anywhere] * 7,
        out_specs=(inside,) * 3,
        scratch_shapes=[
            pltpu.VMEM(queries.shape, BF16),
            pltpu.VMEM(keys.shape, BF16),
            pltpu.VMEM(keys.shape, BF16),
            pltpu.VMEM(queries.shape, BF16),
            pltpu.VMEM((2,) + hidden.shape, BF16),
            pltpu.VMEM((length, width), jnp.int32),
            pltpu.VMEM((rows, length, width), F32),
            pltpu.VMEM((tokens, HD), F32),
            pltpu.SMEM(group_alive.shape, jnp.int32),
            pltpu.SMEM(positions.shape, jnp.int32),
            pltpu.VMEM((2, piece, tokens), BF16),
            pltpu.VMEM((2 * piece, tokens), BF16),
            pltpu.VMEM((N, 2 * piece, tokens), BF16),
            pltpu.VMEM((2, N, piece, tokens), BF16),
            pltpu.VMEM((2, 2, 2, piece, cols), F32),
            pltpu.VMEM((2, 2, 4, 2, piece, cols), BF16),
            pltpu.VMEM((2, 2, 4, 2, piece, cols), BF16),
            pltpu.VMEM((N, 16, cols), BF16),
            pltpu.VMEM((N, 16, cols), BF16),
            pltpu.VMEM((2, 8, cols), F32),
            pltpu.VMEM((2, 8, cols), F32),
            dma((2 * rows + 5,)),
            dma((2,)),
            dma((2, N // 2)),
            dma((2, N)),
            dma((N // 2,)),
            dma((N,)),
            dma((2, 2, 4)),
            dma((2, 2, 4)),
            dma((N,)),
            dma((N,)),
            dma((2,)),
            dma((2,)),
        ],
        compiler_params=pltpu.CompilerParams(
            collective_id=0, has_side_effects=True, vmem_limit_bytes=40 * 1024 * 1024
        ),
        cost_estimate=pl.CostEstimate(
            flops=10 * width * length * HD * rows + 2 * tokens * 1024 * cols,
            bytes_accessed=4000000,
            transcendentals=rows * width * length,
        ),
    )(*(pltpu.with_memory_space_constraint(x, pltpu.HBM) for x in inputs))


def solution(mesh):
    return jax.shard_map(
        local,
        mesh=mesh,
        in_specs=(
            P("dp", None, "tensor"),
            P("dp", None, "tensor"),
            P("dp", None, "tensor"),
            P("dp", None, "tensor"),
            P("dp", None, "tensor"),
            P(),
            P("dp", None),
        ),
        out_specs=(P("dp", None, "tensor"), P("dp", None, "tensor"), P("dp", "tensor")),
        check_vma=False,
    )
```

```python
import jax
import jax.numpy as jnp
from jax import lax
from jax.experimental import pallas as pl
from jax.experimental.pallas import tpu as pltpu
from jax.sharding import PartitionSpec as P

HD = 128
GROUP = 2
N = 8
MESH = pl.DeviceIdType.MESH
F32 = jnp.float32
BF16 = jnp.bfloat16


def contract(a, b, dims):
    return lax.dot_general(a, b, ((dims[:1], dims[1:]), ((), ())), preferred_element_type=F32)


def heads_to_rows(x):
    return jnp.concatenate([x[:, h * HD : (h + 1) * HD] for h in range(x.shape[1] // HD)], axis=0)


def kernel(
    q_hbm, k_hbm, v_hbm, h_hbm, g_hbm, alive_hbm, pos_hbm,
    dq_ref, dk_ref, gw_ref,
    q_buf, k_buf, v_buf, g_buf, h_buf, mask_buf, p_buf, gv_buf, alive_ref, pos_ref,
    gv_half, gv_whole, gv_recv, gv_chunk, part, r_send, r_recv, s2_send, s2_recv, s3_send, s3_recv,
    in_sem, h_sem, gs_sem, gr_sem, ws_sem, wr_sem, rs_sem, rr_sem, s2s_sem, s2r_sem, s3s_sem, s3r_sem,
):
    rows, length, _ = q_buf.shape
    cols = h_buf.shape[-1]
    heads = q_buf.shape[-1] // HD
    width = heads * length
    tokens = rows * length
    factor = HD**-0.5
    piece = HD // 4

    dp = lax.axis_index("dp")
    tensor = lax.axis_index("tensor")
    core = lax.rem(tensor, 2)
    x_hi = lax.rem(dp, 2)
    y = lax.rem(dp // 2, N)
    z = dp // (2 * N)
    stride = 2 * N - (2 * N - 2) * core
    ring = z * (1 - core) + y * core
    stride2 = 2 + (2 * N - 2) * core
    ring2 = y * (1 - core) + z * core

    def on_ring(d):
        return dp + (lax.rem(ring + d + N, N) - ring) * stride

    def at_ring2(place):
        return dp + (place - ring2) * stride2

    far = dp + 1 - 2 * x_hi
    peers = [(far, tensor), (far, tensor + 1 - 2 * core)]
    peers += [(at_ring2(lax.rem(ring2 + d, N)), tensor) for d in range(1, N)]
    peers += [(dp, lax.rem(tensor + d, N)) for d in range(1, N)]
    peers += [(on_ring(d), tensor) for d in (2, -2, 1, -1)]
    barrier = pltpu.get_barrier_semaphore()
    for peer in peers:
        pl.semaphore_signal(barrier, inc=1, device_id=peer, device_id_type=MESH)

    load_scalars = (
        pltpu.make_async_copy(alive_hbm, alive_ref, in_sem.at[2 * rows + 3]),
        pltpu.make_async_copy(pos_hbm, pos_ref, in_sem.at[2 * rows + 4]),
    )

    def load_row(r):
        return (
            pltpu.make_async_copy(q_hbm.at[r], q_buf.at[r], in_sem.at[r]),
            pltpu.make_async_copy(g_hbm.at[r], g_buf.at[r], in_sem.at[rows + r]),
        )

    load_k = pltpu.make_async_copy(k_hbm, k_buf, in_sem.at[2 * rows])
    load_v = pltpu.make_async_copy(v_hbm, v_buf, in_sem.at[2 * rows + 1])
    load_h = pltpu.make_async_copy(h_hbm, h_buf.at[core], in_sem.at[2 * rows + 2])
    for copy in load_scalars:
        copy.start()
    load_k.start()
    for r in range(rows):
        for copy in load_row(r):
            copy.start()
    load_v.start()
    load_h.start()

    k_index = lax.broadcasted_iota(jnp.int32, (length, width), 0)
    lane = lax.broadcasted_iota(jnp.int32, (length, width), 1)
    q_index = lane
    for h in range(1, heads):
        q_index = jnp.where(lane >= h * length, lane - h * length, q_index)
    mask_buf[...] = jnp.where(k_index < q_index, k_index, jnp.where(k_index == q_index, length, -1))

    def masked_grad(r):
        alive = alive_ref[dp * (rows // GROUP) + r // GROUP].astype(F32).astype(BF16)
        return heads_to_rows(g_buf[r] * alive)

    for copy in load_scalars:
        copy.wait()
    load_k.wait()

    def forward(r, carry):
        for copy in load_row(r):
            copy.wait()
        queries = heads_to_rows(q_buf[r])
        grads = masked_grad(r)
        scores = contract(k_buf[r], queries, (1, 1)) * factor
        scores = jnp.where(mask_buf[...] >= -pos_ref[r, 0], scores, F32(-1e30))
        expo = jnp.exp(scores - jnp.max(scores, axis=0, keepdims=True))
        probs = expo * (1.0 / jnp.sum(expo, axis=0, keepdims=True))
        p_buf[r] = probs
        at = pl.ds(pl.multiple_of(r * length, length), length)
        gv_buf[at, :] = contract(probs.astype(BF16), grads, (1, 0))
        return carry

    lax.fori_loop(0, rows, forward, 0)

    value_grad = gv_buf[...].T.reshape(HD // 16, 2, 8, tokens)
    for s in range(2):
        gv_half[s] = value_grad[4 * s : 4 * s + 4, 0].reshape(piece, tokens).astype(BF16)
    gv_whole[...] = value_grad[:, 1].reshape(2 * piece, tokens).astype(BF16)

    pl.semaphore_wait(barrier, len(peers))

    def give_half(s, chip):
        return pltpu.make_async_remote_copy(
            src_ref=gv_half.at[s], dst_ref=gv_chunk.at[s, tensor],
            send_sem=gs_sem.at[s, chip], recv_sem=gr_sem.at[s, tensor],
            device_id=(dp, 2 * chip), device_id_type=MESH,
        )

    def take_half(s, of):
        return pltpu.make_async_remote_copy(
            src_ref=gv_half.at[s], dst_ref=gv_chunk.at[s, of],
            send_sem=gs_sem.at[s, 0], recv_sem=gr_sem.at[s, of],
            device_id=(dp, of), device_id_type=MESH,
        )

    def give_whole(chip):
        return pltpu.make_async_remote_copy(
            src_ref=gv_whole, dst_ref=gv_recv.at[tensor],
            send_sem=ws_sem.at[chip], recv_sem=wr_sem.at[tensor],
            device_id=(dp, 2 * chip + 1), device_id_type=MESH,
        )

    def take_whole(of):
        return pltpu.make_async_remote_copy(
            src_ref=gv_whole, dst_ref=gv_recv.at[of],
            send_sem=ws_sem.at[0], recv_sem=wr_sem.at[of],
            device_id=(dp, of), device_id_type=MESH,
        )

    chips = N // 2
    own = tensor // 2
    away = [lax.rem(own + d, chips) for d in (2, 1, 3)]
    for s in range(2):
        for chip in away:
            give_half(s, chip).start()

        @pl.when(core == s)
        def _():
            for chip in away:
                give_whole(chip).start()

        @pl.when(core == 1)
        def _():
            give_half(s, own).start()

    @pl.when(core == 0)
    def _():
        give_whole(own).start()
        for s in range(2):
            gv_chunk[s, tensor] = gv_half[s]

    @pl.when(core == 1)
    def _():
        gv_recv[tensor] = gv_whole[...]

    swap_h = pltpu.make_async_remote_copy(
        src_ref=h_hbm, dst_ref=h_buf.at[core], send_sem=h_sem.at[0], recv_sem=h_sem.at[1],
        device_id=(dp, tensor + 1 - 2 * core), device_id_type=MESH,
    )
    swap_h.start()
    load_v.wait()

    def backward(r, carry):
        queries = heads_to_rows(q_buf[r])
        grads = masked_grad(r)
        probs = p_buf[r]
        dprobs = contract(v_buf[r], grads, (1, 1))
        delta = jnp.sum(probs.astype(BF16).astype(F32) * dprobs, axis=0, keepdims=True)
        dscores = (probs * (dprobs - delta)).astype(BF16)
        dk_ref[r] = (contract(dscores, queries, (1, 0)) * factor).astype(BF16)
        dq = (contract(dscores, k_buf[r], (0, 0)) * factor).astype(BF16)
        for h in range(heads):
            dq_ref[r, :, h * HD : (h + 1) * HD] = dq[h * length : (h + 1) * length]
        return carry

    lax.fori_loop(0, rows, backward, 0)
    load_h.wait()
    swap_h.wait_recv()

    def gathered(s):
        @pl.when(core == 0)
        def _():
            for d in range(1, N):
                take_half(s, lax.rem(tensor + d, N)).wait_recv()

        @pl.when(core == 1)
        def _():
            for chip in range(chips):
                of = 2 * chip + s

                @pl.when(of != tensor)
                def _():
                    take_whole(of).wait_recv()

            parts = [gv_recv[2 * chip + s].astype(F32) for chip in range(chips)]
            for t in range(N):
                gv_chunk[s, t] = jnp.concatenate([x[8 * t : 8 * t + 8] for x in parts], axis=0).astype(BF16)

    def products(s, offsets):
        left = jnp.concatenate([gv_chunk[s, lax.rem(ring + d + N, N)] for d in offsets], axis=0)
        for k in range(2):
            both = contract(left, h_buf[k].reshape(tokens, cols), (1, 0))
            for i in range(len(offsets)):
                part[s, i, k] = both[i * piece : (i + 1) * piece]

    def hop(way, s, j):
        return pltpu.make_async_remote_copy(
            src_ref=r_send.at[way, s, j], dst_ref=r_recv.at[way, s, j],
            send_sem=rs_sem.at[way, s, j], recv_sem=rr_sem.at[way, s, j],
            device_id=(on_ring((1 if j else 2) * (1 - 2 * way)), tensor), device_id_type=MESH,
        )

    def first_sends(s):
        products(s, (3, -3, 4))
        r_send[s, s, 0] = part[s, 2].astype(BF16)
        hop(s, s, 0).start()
        for way in (s, 1 - s):
            r_send[way, s, 1] = part[s, way].astype(BF16)
            hop(way, s, 1).start()
        products(s, (2, -2))

    def pass_on(way, s, j):
        total = part[s, way]
        for k in ((0, 1) if j == 2 and way == s else (j - 1,)):
            hop(way, s, k).wait_recv()
            total = total + r_recv[way, s, k].astype(F32)
        r_send[way, s, j] = total.astype(BF16)
        hop(way, s, j).start()

    def second_sends(s):
        for way in (1 - s, s):
            pass_on(way, s, 2)
        products(s, (1, -1))

    def last_sends(s):
        for way in (1 - s, s):
            pass_on(way, s, 3)
        products(s, (0,))

    def place2(i):
        return i * (1 - core) + (2 * (i % 4) + i // 4) * core

    def cross(i):
        return pltpu.make_async_remote_copy(
            src_ref=s2_send.at[i], dst_ref=s2_recv.at[ring2],
            send_sem=s2s_sem.at[i], recv_sem=s2r_sem.at[ring2],
            device_id=(at_ring2(place2(i)), tensor), device_id_type=MESH,
        )

    def cross_in(of):
        return pltpu.make_async_remote_copy(
            src_ref=s2_send.at[0], dst_ref=s2_recv.at[of],
            send_sem=s2s_sem.at[0], recv_sem=s2r_sem.at[of],
            device_id=(at_ring2(of), tensor), device_id_type=MESH,
        )

    def if_away(i, act):
        @pl.when(place2(i) != ring2)
        def _():
            act(cross(i))

    def ring_end(s):
        total = part[s, 0]
        for way in (1 - s, s):
            hop(way, s, 3).wait_recv()
            total = total + r_recv[way, s, 3].astype(F32)
        total = total.reshape(2, 4, 8, cols)
        s2_send[4 * s : 4 * s + 4] = jnp.concatenate([total[0], total[1]], axis=1).astype(BF16)
        for i in range(4 * s, 4 * s + 4):
            if_away(i, lambda copy: copy.start())

    gathered(0)
    first_sends(0)
    second_sends(0)
    gathered(1)
    first_sends(1)
    last_sends(0)
    second_sends(1)
    last_sends(1)
    ring_end(0)
    ring_end(1)

    for s in range(2):
        for chip in away:
            give_half(s, chip).wait_send()
        for way in range(2):
            for j in range(0 if way == s else 1, 4):
                hop(way, s, j).wait_send()
    for chip in away:
        give_whole(chip).wait_send()

    @pl.when(core == 0)
    def _():
        give_whole(own).wait_send()

    @pl.when(core == 1)
    def _():
        for s in range(2):
            give_half(s, own).wait_send()

    swap_h.wait_send()

    mine = ring2 * (1 - core) + (ring2 // 2 + 4 * lax.rem(ring2, 2)) * core
    total = s2_send[mine].astype(F32)
    for d in (1, 7, 2, 6, 3, 5, 4):
        of = lax.rem(ring2 + d, N)
        cross_in(of).wait_recv()
        total = total + s2_recv[of].astype(F32)
    for k in range(2):
        s3_send[k] = total[8 * k : 8 * k + 8]

    def finish(k):
        return pltpu.make_async_remote_copy(
            src_ref=s3_send.at[k], dst_ref=s3_recv.at[x_hi],
            send_sem=s3s_sem.at[k], recv_sem=s3r_sem.at[x_hi],
            device_id=(dp - x_hi + core, tensor - core + k), device_id_type=MESH,
        )

    def finish_in(of):
        return pltpu.make_async_remote_copy(
            src_ref=s3_send.at[0], dst_ref=s3_recv.at[of],
            send_sem=s3s_sem.at[0], recv_sem=s3r_sem.at[of],
            device_id=(far, tensor), device_id_type=MESH,
        )

    home = x_hi == core

    @pl.when(home)
    def _():
        finish(1 - core).start()

    @pl.when(jnp.logical_not(home))
    def _():
        for k in range(2):
            finish(k).start()

    for i in range(N):
        if_away(i, lambda copy: copy.wait_send())

    @pl.when(home)
    def _():
        finish_in(1 - x_hi).wait_recv()
        gw_ref[...] = s3_send[core] + s3_recv[1 - x_hi]
        finish(1 - core).wait_send()

    @pl.when(jnp.logical_not(home))
    def _():
        for of in range(2):
            finish_in(of).wait_recv()
        gw_ref[...] = s3_recv[0] + s3_recv[1]
        for k in range(2):
            finish(k).wait_send()


def local(queries, keys, values, hidden, grad_out, group_alive, positions):
    rows, length, model = queries.shape
    cols = hidden.shape[-1]
    heads = model // HD
    width = heads * length
    tokens = rows * length
    piece = HD // 4
    anywhere = pl.BlockSpec(memory_space=pl.ANY)
    inside = pl.BlockSpec(memory_space=pltpu.VMEM)
    dma = pltpu.SemaphoreType.DMA
    inputs = (queries, keys, values, hidden, grad_out, group_alive, positions)
    return pl.pallas_call(
        kernel,
        out_shape=(
            pltpu.VMEM(queries.shape, BF16),
            pltpu.VMEM(keys.shape, BF16),
            pltpu.VMEM((8, cols), F32),
        ),
        in_specs=[anywhere] * 7,
        out_specs=(inside,) * 3,
        scratch_shapes=[
            pltpu.VMEM(queries.shape, BF16),
            pltpu.VMEM(keys.shape, BF16),
            pltpu.VMEM(keys.shape, BF16),
            pltpu.VMEM(queries.shape, BF16),
            pltpu.VMEM((2,) + hidden.shape, BF16),
            pltpu.VMEM((length, width), jnp.int32),
            pltpu.VMEM((rows, length, width), F32),
            pltpu.VMEM((tokens, HD), F32),
            pltpu.SMEM(group_alive.shape, jnp.int32),
            pltpu.SMEM(positions.shape, jnp.int32),
            pltpu.VMEM((2, piece, tokens), BF16),
            pltpu.VMEM((2 * piece, tokens), BF16),
            pltpu.VMEM((N, 2 * piece, tokens), BF16),
            pltpu.VMEM((2, N, piece, tokens), BF16),
            pltpu.VMEM((2, 3, 2, piece, cols), F32),
            pltpu.VMEM((2, 2, 4, 2, piece, cols), BF16),
            pltpu.VMEM((2, 2, 4, 2, piece, cols), BF16),
            pltpu.VMEM((N, 16, cols), BF16),
            pltpu.VMEM((N, 16, cols), BF16),
            pltpu.VMEM((2, 8, cols), F32),
            pltpu.VMEM((2, 8, cols), F32),
            dma((2 * rows + 5,)),
            dma((2,)),
            dma((2, N // 2)),
            dma((2, N)),
            dma((N // 2,)),
            dma((N,)),
            dma((2, 2, 4)),
            dma((2, 2, 4)),
            dma((N,)),
            dma((N,)),
            dma((2,)),
            dma((2,)),
        ],
        compiler_params=pltpu.CompilerParams(
            collective_id=0, has_side_effects=True, vmem_limit_bytes=40 * 1024 * 1024
        ),
        cost_estimate=pl.CostEstimate(
            flops=10 * width * length * HD * rows + 2 * tokens * 1024 * cols,
            bytes_accessed=4000000,
            transcendentals=rows * width * length,
        ),
    )(*(pltpu.with_memory_space_constraint(x, pltpu.HBM) for x in inputs))


def solution(mesh):
    return jax.shard_map(
        local,
        mesh=mesh,
        in_specs=(
            P("dp", None, "tensor"),
            P("dp", None, "tensor"),
            P("dp", None, "tensor"),
            P("dp", None, "tensor"),
            P("dp", None, "tensor"),
            P(),
            P("dp", None),
        ),
        out_specs=(P("dp", None, "tensor"), P("dp", None, "tensor"), P("dp", "tensor")),
        check_vma=False,
    )
```

```python
import jax
import jax.numpy as jnp
from jax import lax
from jax.experimental import pallas as pl
from jax.experimental.pallas import tpu as pltpu
from jax.sharding import PartitionSpec as P

HD = 128
GROUP = 2
N = 8
MESH = pl.DeviceIdType.MESH
F32 = jnp.float32
BF16 = jnp.bfloat16


def contract(a, b, dims):
    return lax.dot_general(a, b, ((dims[:1], dims[1:]), ((), ())), preferred_element_type=F32)


def heads_to_rows(x):
    return jnp.concatenate([x[:, h * HD : (h + 1) * HD] for h in range(x.shape[1] // HD)], axis=0)


def kernel(
    q_hbm, k_hbm, v_hbm, h_hbm, g_hbm, alive_hbm, pos_hbm,
    dq_ref, dk_ref, gw_ref,
    q_buf, k_buf, v_buf, g_buf, h_buf, mask_buf, p_buf, gv_buf, alive_ref, pos_ref,
    gv_half, gv_whole, gv_recv, gv_chunk, part, r_send, r_recv, s2_send, s2_recv, s3_send, s3_recv,
    in_sem, h_sem, gs_sem, gr_sem, ws_sem, wr_sem, rs_sem, rr_sem, s2s_sem, s2r_sem, s3s_sem, s3r_sem,
):
    rows, length, _ = q_buf.shape
    cols = h_buf.shape[-1]
    heads = q_buf.shape[-1] // HD
    width = heads * length
    tokens = rows * length
    factor = HD**-0.5
    piece = HD // 4

    dp = lax.axis_index("dp")
    tensor = lax.axis_index("tensor")
    core = lax.rem(tensor, 2)
    x_hi = lax.rem(dp, 2)
    y = lax.rem(dp // 2, N)
    z = dp // (2 * N)
    stride = 2 * N - (2 * N - 2) * core
    ring = z * (1 - core) + y * core
    stride2 = 2 + (2 * N - 2) * core
    ring2 = y * (1 - core) + z * core

    def on_ring(d):
        return dp + (lax.rem(ring + d + N, N) - ring) * stride

    def at_ring2(place):
        return dp + (place - ring2) * stride2

    far = dp + 1 - 2 * x_hi
    peers = [(far, tensor), (far, tensor + 1 - 2 * core)]
    peers += [(at_ring2(lax.rem(ring2 + d, N)), tensor) for d in range(1, N)]
    peers += [(dp, lax.rem(tensor + d, N)) for d in range(1, N)]
    peers += [(on_ring(d), tensor) for d in (2, -2, 1, -1)]
    barrier = pltpu.get_barrier_semaphore()
    for peer in peers:
        pl.semaphore_signal(barrier, inc=1, device_id=peer, device_id_type=MESH)

    load_scalars = (
        pltpu.make_async_copy(alive_hbm, alive_ref, in_sem.at[2 * rows + 3]),
        pltpu.make_async_copy(pos_hbm, pos_ref, in_sem.at[2 * rows + 4]),
    )

    def load_row(r):
        return (
            pltpu.make_async_copy(q_hbm.at[r], q_buf.at[r], in_sem.at[r]),
            pltpu.make_async_copy(g_hbm.at[r], g_buf.at[r], in_sem.at[rows + r]),
        )

    load_k = pltpu.make_async_copy(k_hbm, k_buf, in_sem.at[2 * rows])
    load_v = pltpu.make_async_copy(v_hbm, v_buf, in_sem.at[2 * rows + 1])
    load_h = pltpu.make_async_copy(h_hbm, h_buf.at[core], in_sem.at[2 * rows + 2])
    for copy in load_scalars:
        copy.start()
    load_k.start()
    for r in range(rows):
        for copy in load_row(r):
            copy.start()
    load_v.start()
    load_h.start()

    k_index = lax.broadcasted_iota(jnp.int32, (length, width), 0)
    lane = lax.broadcasted_iota(jnp.int32, (length, width), 1)
    q_index = lane
    for h in range(1, heads):
        q_index = jnp.where(lane >= h * length, lane - h * length, q_index)
    mask_buf[...] = jnp.where(k_index < q_index, k_index, jnp.where(k_index == q_index, length, -1))

    def masked_grad(r):
        alive = alive_ref[dp * (rows // GROUP) + r // GROUP].astype(F32).astype(BF16)
        return heads_to_rows(g_buf[r] * alive)

    for copy in load_scalars:
        copy.wait()
    load_k.wait()

    def forward(r, carry):
        for copy in load_row(r):
            copy.wait()
        queries = heads_to_rows(q_buf[r])
        grads = masked_grad(r)
        scores = contract(k_buf[r], queries, (1, 1)) * factor
        scores = jnp.where(mask_buf[...] >= -pos_ref[r, 0], scores, F32(-1e30))
        expo = jnp.exp(scores - jnp.max(scores, axis=0, keepdims=True))
        probs = expo * (1.0 / jnp.sum(expo, axis=0, keepdims=True))
        p_buf[r] = probs
        at = pl.ds(pl.multiple_of(r * length, length), length)
        gv_buf[at, :] = contract(probs.astype(BF16), grads, (1, 0))
        return carry

    lax.fori_loop(0, rows, forward, 0)

    value_grad = gv_buf[...].T.reshape(HD // 16, 2, 8, tokens)
    for s in range(2):
        gv_half[s] = value_grad[4 * s : 4 * s + 4, 0].reshape(piece, tokens).astype(BF16)
    gv_whole[...] = value_grad[:, 1].reshape(2 * piece, tokens).astype(BF16)

    pl.semaphore_wait(barrier, len(peers))

    def give_half(s, chip):
        return pltpu.make_async_remote_copy(
            src_ref=gv_half.at[s], dst_ref=gv_chunk.at[s, tensor],
            send_sem=gs_sem.at[s, chip], recv_sem=gr_sem.at[s, tensor],
            device_id=(dp, 2 * chip), device_id_type=MESH,
        )

    def take_half(s, of):
        return pltpu.make_async_remote_copy(
            src_ref=gv_half.at[s], dst_ref=gv_chunk.at[s, of],
            send_sem=gs_sem.at[s, 0], recv_sem=gr_sem.at[s, of],
            device_id=(dp, of), device_id_type=MESH,
        )

    def give_whole(chip):
        return pltpu.make_async_remote_copy(
            src_ref=gv_whole, dst_ref=gv_recv.at[tensor],
            send_sem=ws_sem.at[chip], recv_sem=wr_sem.at[tensor],
            device_id=(dp, 2 * chip + 1), device_id_type=MESH,
        )

    def take_whole(of):
        return pltpu.make_async_remote_copy(
            src_ref=gv_whole, dst_ref=gv_recv.at[of],
            send_sem=ws_sem.at[0], recv_sem=wr_sem.at[of],
            device_id=(dp, of), device_id_type=MESH,
        )

    chips = N // 2
    own = tensor // 2
    away = [lax.rem(own + d, chips) for d in (2, 1, 3)]
    for s in range(2):
        for chip in away:
            give_half(s, chip).start()

        @pl.when(core == s)
        def _():
            for chip in away:
                give_whole(chip).start()

        @pl.when(core == 1)
        def _():
            give_half(s, own).start()

    @pl.when(core == 0)
    def _():
        give_whole(own).start()
        for s in range(2):
            gv_chunk[s, tensor] = gv_half[s]

    @pl.when(core == 1)
    def _():
        gv_recv[tensor] = gv_whole[...]

    swap_h = pltpu.make_async_remote_copy(
        src_ref=h_hbm, dst_ref=h_buf.at[core], send_sem=h_sem.at[0], recv_sem=h_sem.at[1],
        device_id=(dp, tensor + 1 - 2 * core), device_id_type=MESH,
    )
    swap_h.start()
    load_v.wait()

    def backward(r, carry):
        queries = heads_to_rows(q_buf[r])
        grads = masked_grad(r)
        probs = p_buf[r]
        dprobs = contract(v_buf[r], grads, (1, 1))
        delta = jnp.sum(probs.astype(BF16).astype(F32) * dprobs, axis=0, keepdims=True)
        dscores = (probs * (dprobs - delta)).astype(BF16)
        dk_ref[r] = (contract(dscores, queries, (1, 0)) * factor).astype(BF16)
        dq = (contract(dscores, k_buf[r], (0, 0)) * factor).astype(BF16)
        for h in range(heads):
            dq_ref[r, :, h * HD : (h + 1) * HD] = dq[h * length : (h + 1) * length]
        return carry

    lax.fori_loop(0, rows, backward, 0)
    load_h.wait()
    swap_h.wait_recv()

    def gathered(s):
        @pl.when(core == 0)
        def _():
            for d in range(1, N):
                take_half(s, lax.rem(tensor + d, N)).wait_recv()

        @pl.when(core == 1)
        def _():
            for chip in range(chips):
                of = 2 * chip + s

                @pl.when(of != tensor)
                def _():
                    take_whole(of).wait_recv()

            parts = [gv_recv[2 * chip + s].astype(F32) for chip in range(chips)]
            for t in range(N):
                gv_chunk[s, t] = jnp.concatenate([x[8 * t : 8 * t + 8] for x in parts], axis=0).astype(BF16)

    def products(s, offsets):
        left = jnp.concatenate([gv_chunk[s, lax.rem(ring + d + N, N)] for d in offsets], axis=0)
        for k in range(2):
            both = contract(left, h_buf[k].reshape(tokens, cols), (1, 0))
            for i in range(len(offsets)):
                part[s, i, k] = both[i * piece : (i + 1) * piece]

    def hop(way, s, j):
        return pltpu.make_async_remote_copy(
            src_ref=r_send.at[way, s, j], dst_ref=r_recv.at[way, s, j],
            send_sem=rs_sem.at[way, s, j], recv_sem=rr_sem.at[way, s, j],
            device_id=(on_ring((1 if j else 2) * (1 - 2 * way)), tensor), device_id_type=MESH,
        )

    def first_sends(s):
        products(s, (3, -3, 4))
        r_send[s, s, 0] = part[s, 2].astype(BF16)
        hop(s, s, 0).start()
        for way in (s, 1 - s):
            r_send[way, s, 1] = part[s, way].astype(BF16)
            hop(way, s, 1).start()
        products(s, (2, -2))

    def pass_on(way, s, j):
        total = part[s, way]
        for k in ((0, 1) if j == 2 and way == s else (j - 1,)):
            hop(way, s, k).wait_recv()
            total = total + r_recv[way, s, k].astype(F32)
        r_send[way, s, j] = total.astype(BF16)
        hop(way, s, j).start()

    def second_sends(s):
        for way in (1 - s, s):
            pass_on(way, s, 2)
        products(s, (1, -1))

    def last_sends(s):
        for way in (1 - s, s):
            pass_on(way, s, 3)
        products(s, (0,))

    def place2(i):
        return i * (1 - core) + (2 * (i % 4) + i // 4) * core

    def cross(i):
        return pltpu.make_async_remote_copy(
            src_ref=s2_send.at[i], dst_ref=s2_recv.at[ring2],
            send_sem=s2s_sem.at[i], recv_sem=s2r_sem.at[ring2],
            device_id=(at_ring2(place2(i)), tensor), device_id_type=MESH,
        )

    def cross_in(of):
        return pltpu.make_async_remote_copy(
            src_ref=s2_send.at[0], dst_ref=s2_recv.at[of],
            send_sem=s2s_sem.at[0], recv_sem=s2r_sem.at[of],
            device_id=(at_ring2(of), tensor), device_id_type=MESH,
        )

    def if_away(i, act):
        @pl.when(place2(i) != ring2)
        def _():
            act(cross(i))

    def ring_end(s):
        total = part[s, 0]
        for way in (1 - s, s):
            hop(way, s, 3).wait_recv()
            total = total + r_recv[way, s, 3].astype(F32)
        total = total.reshape(2, 4, 8, cols)
        s2_send[4 * s : 4 * s + 4] = jnp.concatenate([total[0], total[1]], axis=1).astype(BF16)
        for i in range(4 * s, 4 * s + 4):
            if_away(i, lambda copy: copy.start())

    gathered(0)
    first_sends(0)
    gathered(1)
    first_sends(1)
    second_sends(0)
    second_sends(1)
    last_sends(0)
    last_sends(1)
    ring_end(0)
    ring_end(1)

    for s in range(2):
        for chip in away:
            give_half(s, chip).wait_send()
        for way in range(2):
            for j in range(0 if way == s else 1, 4):
                hop(way, s, j).wait_send()
    for chip in away:
        give_whole(chip).wait_send()

    @pl.when(core == 0)
    def _():
        give_whole(own).wait_send()

    @pl.when(core == 1)
    def _():
        for s in range(2):
            give_half(s, own).wait_send()

    swap_h.wait_send()

    mine = ring2 * (1 - core) + (ring2 // 2 + 4 * lax.rem(ring2, 2)) * core
    total = s2_send[mine].astype(F32)
    for d in (1, 7, 2, 6, 3, 5, 4):
        of = lax.rem(ring2 + d, N)
        cross_in(of).wait_recv()
        total = total + s2_recv[of].astype(F32)
    for k in range(2):
        s3_send[k] = total[8 * k : 8 * k + 8]

    def finish(k):
        return pltpu.make_async_remote_copy(
            src_ref=s3_send.at[k], dst_ref=s3_recv.at[x_hi],
            send_sem=s3s_sem.at[k], recv_sem=s3r_sem.at[x_hi],
            device_id=(dp - x_hi + core, tensor - core + k), device_id_type=MESH,
        )

    def finish_in(of):
        return pltpu.make_async_remote_copy(
            src_ref=s3_send.at[0], dst_ref=s3_recv.at[of],
            send_sem=s3s_sem.at[0], recv_sem=s3r_sem.at[of],
            device_id=(far, tensor), device_id_type=MESH,
        )

    home = x_hi == core

    @pl.when(home)
    def _():
        finish(1 - core).start()

    @pl.when(jnp.logical_not(home))
    def _():
        for k in range(2):
            finish(k).start()

    for i in range(N):
        if_away(i, lambda copy: copy.wait_send())

    @pl.when(home)
    def _():
        finish_in(1 - x_hi).wait_recv()
        gw_ref[...] = s3_send[core] + s3_recv[1 - x_hi]
        finish(1 - core).wait_send()

    @pl.when(jnp.logical_not(home))
    def _():
        for of in range(2):
            finish_in(of).wait_recv()
        gw_ref[...] = s3_recv[0] + s3_recv[1]
        for k in range(2):
            finish(k).wait_send()


def local(queries, keys, values, hidden, grad_out, group_alive, positions):
    rows, length, model = queries.shape
    cols = hidden.shape[-1]
    heads = model // HD
    width = heads * length
    tokens = rows * length
    piece = HD // 4
    anywhere = pl.BlockSpec(memory_space=pl.ANY)
    inside = pl.BlockSpec(memory_space=pltpu.VMEM)
    dma = pltpu.SemaphoreType.DMA
    inputs = (queries, keys, values, hidden, grad_out, group_alive, positions)
    return pl.pallas_call(
        kernel,
        out_shape=(
            pltpu.VMEM(queries.shape, BF16),
            pltpu.VMEM(keys.shape, BF16),
            pltpu.VMEM((8, cols), F32),
        ),
        in_specs=[anywhere] * 7,
        out_specs=(inside,) * 3,
        scratch_shapes=[
            pltpu.VMEM(queries.shape, BF16),
            pltpu.VMEM(keys.shape, BF16),
            pltpu.VMEM(keys.shape, BF16),
            pltpu.VMEM(queries.shape, BF16),
            pltpu.VMEM((2,) + hidden.shape, BF16),
            pltpu.VMEM((length, width), jnp.int32),
            pltpu.VMEM((rows, length, width), F32),
            pltpu.VMEM((tokens, HD), F32),
            pltpu.SMEM(group_alive.shape, jnp.int32),
            pltpu.SMEM(positions.shape, jnp.int32),
            pltpu.VMEM((2, piece, tokens), BF16),
            pltpu.VMEM((2 * piece, tokens), BF16),
            pltpu.VMEM((N, 2 * piece, tokens), BF16),
            pltpu.VMEM((2, N, piece, tokens), BF16),
            pltpu.VMEM((2, 3, 2, piece, cols), F32),
            pltpu.VMEM((2, 2, 4, 2, piece, cols), BF16),
            pltpu.VMEM((2, 2, 4, 2, piece, cols), BF16),
            pltpu.VMEM((N, 16, cols), BF16),
            pltpu.VMEM((N, 16, cols), BF16),
            pltpu.VMEM((2, 8, cols), F32),
            pltpu.VMEM((2, 8, cols), F32),
            dma((2 * rows + 5,)),
            dma((2,)),
            dma((2, N // 2)),
            dma((2, N)),
            dma((N // 2,)),
            dma((N,)),
            dma((2, 2, 4)),
            dma((2, 2, 4)),
            dma((N,)),
            dma((N,)),
            dma((2,)),
            dma((2,)),
        ],
        compiler_params=pltpu.CompilerParams(
            collective_id=0, has_side_effects=True, vmem_limit_bytes=40 * 1024 * 1024
        ),
        cost_estimate=pl.CostEstimate(
            flops=10 * width * length * HD * rows + 2 * tokens * 1024 * cols,
            bytes_accessed=4000000,
            transcendentals=rows * width * length,
        ),
    )(*(pltpu.with_memory_space_constraint(x, pltpu.HBM) for x in inputs))


def solution(mesh):
    return jax.shard_map(
        local,
        mesh=mesh,
        in_specs=(
            P("dp", None, "tensor"),
            P("dp", None, "tensor"),
            P("dp", None, "tensor"),
            P("dp", None, "tensor"),
            P("dp", None, "tensor"),
            P(),
            P("dp", None),
        ),
        out_specs=(P("dp", None, "tensor"), P("dp", None, "tensor"), P("dp", "tensor")),
        check_vma=False,
    )
```

```python
import jax
import jax.numpy as jnp
from jax import lax
from jax.experimental import pallas as pl
from jax.experimental.pallas import tpu as pltpu
from jax.sharding import PartitionSpec as P

HD = 128
GROUP = 2
N = 8
MESH = pl.DeviceIdType.MESH
F32 = jnp.float32
BF16 = jnp.bfloat16


def contract(a, b, dims):
    return lax.dot_general(a, b, ((dims[:1], dims[1:]), ((), ())), preferred_element_type=F32)


def heads_to_rows(x):
    return jnp.concatenate([x[:, h * HD : (h + 1) * HD] for h in range(x.shape[1] // HD)], axis=0)


def kernel(
    q_hbm, k_hbm, v_hbm, h_hbm, g_hbm, alive_hbm, pos_hbm,
    dq_ref, dk_ref, gw_ref,
    q_buf, k_buf, v_buf, g_buf, h_buf, mask_buf, p_buf, gv_buf, alive_ref, pos_ref,
    gv_half, gv_whole, gv_recv, gv_chunk, part, r_send, r_recv, s2_send, s2_recv, s3_send, s3_recv,
    in_sem, h_sem, gs_sem, gr_sem, ws_sem, wr_sem, rs_sem, rr_sem, s2s_sem, s2r_sem, s3s_sem, s3r_sem,
):
    rows, length, _ = q_buf.shape
    cols = h_buf.shape[-1]
    heads = q_buf.shape[-1] // HD
    width = heads * length
    tokens = rows * length
    factor = HD**-0.5
    piece = HD // 4

    dp = lax.axis_index("dp")
    tensor = lax.axis_index("tensor")
    core = lax.rem(tensor, 2)
    x_hi = lax.rem(dp, 2)
    y = lax.rem(dp // 2, N)
    z = dp // (2 * N)
    stride = 2 * N - (2 * N - 2) * core
    ring = z * (1 - core) + y * core
    stride2 = 2 + (2 * N - 2) * core
    ring2 = y * (1 - core) + z * core

    def on_ring(d):
        return dp + (lax.rem(ring + d + N, N) - ring) * stride

    def at_ring2(place):
        return dp + (place - ring2) * stride2

    far = dp + 1 - 2 * x_hi
    peers = [(far, tensor), (far, tensor + 1 - 2 * core)]
    peers += [(at_ring2(lax.rem(ring2 + d, N)), tensor) for d in range(1, N)]
    peers += [(dp, lax.rem(tensor + d, N)) for d in range(1, N)]
    peers += [(on_ring(d), tensor) for d in (2, -2, 1, -1)]
    barrier = pltpu.get_barrier_semaphore()
    for peer in peers:
        pl.semaphore_signal(barrier, inc=1, device_id=peer, device_id_type=MESH)

    load_scalars = (
        pltpu.make_async_copy(alive_hbm, alive_ref, in_sem.at[2 * rows + 3]),
        pltpu.make_async_copy(pos_hbm, pos_ref, in_sem.at[2 * rows + 4]),
    )

    def load_row(r):
        return (
            pltpu.make_async_copy(q_hbm.at[r], q_buf.at[r], in_sem.at[r]),
            pltpu.make_async_copy(g_hbm.at[r], g_buf.at[r], in_sem.at[rows + r]),
        )

    load_k = pltpu.make_async_copy(k_hbm, k_buf, in_sem.at[2 * rows])
    load_v = pltpu.make_async_copy(v_hbm, v_buf, in_sem.at[2 * rows + 1])
    load_h = pltpu.make_async_copy(h_hbm, h_buf.at[core], in_sem.at[2 * rows + 2])
    for copy in load_scalars:
        copy.start()
    load_k.start()
    for r in range(rows):
        for copy in load_row(r):
            copy.start()
    load_v.start()
    load_h.start()

    k_index = lax.broadcasted_iota(jnp.int32, (length, width), 0)
    lane = lax.broadcasted_iota(jnp.int32, (length, width), 1)
    q_index = lane
    for h in range(1, heads):
        q_index = jnp.where(lane >= h * length, lane - h * length, q_index)
    mask_buf[...] = jnp.where(k_index < q_index, k_index, jnp.where(k_index == q_index, length, -1))

    def masked_grad(r):
        alive = alive_ref[dp * (rows // GROUP) + r // GROUP].astype(F32).astype(BF16)
        return heads_to_rows(g_buf[r] * alive)

    for copy in load_scalars:
        copy.wait()
    load_k.wait()

    def forward(r, carry):
        for copy in load_row(r):
            copy.wait()
        queries = heads_to_rows(q_buf[r])
        grads = masked_grad(r)
        scores = contract(k_buf[r], queries, (1, 1)) * factor
        scores = jnp.where(mask_buf[...] >= -pos_ref[r, 0], scores, F32(-1e30))
        expo = jnp.exp(scores - jnp.max(scores, axis=0, keepdims=True))
        probs = expo * (1.0 / jnp.sum(expo, axis=0, keepdims=True))
        p_buf[r] = probs
        at = pl.ds(pl.multiple_of(r * length, length), length)
        gv_buf[at, :] = contract(probs.astype(BF16), grads, (1, 0))
        return carry

    lax.fori_loop(0, rows, forward, 0)

    value_grad = gv_buf[...].T.reshape(HD // 16, 2, 8, tokens)
    for s in range(2):
        gv_half[s] = value_grad[4 * s : 4 * s + 4, 0].reshape(piece, tokens).astype(BF16)
    gv_whole[...] = value_grad[:, 1].reshape(2 * piece, tokens).astype(BF16)

    pl.semaphore_wait(barrier, len(peers))

    def give_half(s, chip):
        return pltpu.make_async_remote_copy(
            src_ref=gv_half.at[s], dst_ref=gv_chunk.at[s, tensor],
            send_sem=gs_sem.at[s, chip], recv_sem=gr_sem.at[s, tensor],
            device_id=(dp, 2 * chip), device_id_type=MESH,
        )

    def take_half(s, of):
        return pltpu.make_async_remote_copy(
            src_ref=gv_half.at[s], dst_ref=gv_chunk.at[s, of],
            send_sem=gs_sem.at[s, 0], recv_sem=gr_sem.at[s, of],
            device_id=(dp, of), device_id_type=MESH,
        )

    def give_whole(chip):
        return pltpu.make_async_remote_copy(
            src_ref=gv_whole, dst_ref=gv_recv.at[tensor],
            send_sem=ws_sem.at[chip], recv_sem=wr_sem.at[tensor],
            device_id=(dp, 2 * chip + 1), device_id_type=MESH,
        )

    def take_whole(of):
        return pltpu.make_async_remote_copy(
            src_ref=gv_whole, dst_ref=gv_recv.at[of],
            send_sem=ws_sem.at[0], recv_sem=wr_sem.at[of],
            device_id=(dp, of), device_id_type=MESH,
        )

    chips = N // 2
    own = tensor // 2
    away = [lax.rem(own + d, chips) for d in (2, 1, 3)]
    for s in range(2):
        for chip in away:
            give_half(s, chip).start()

        @pl.when(core == s)
        def _():
            for chip in away:
                give_whole(chip).start()

        @pl.when(core == 1)
        def _():
            give_half(s, own).start()

    @pl.when(core == 0)
    def _():
        give_whole(own).start()
        for s in range(2):
            gv_chunk[s, tensor] = gv_half[s]

    @pl.when(core == 1)
    def _():
        gv_recv[tensor] = gv_whole[...]

    swap_h = pltpu.make_async_remote_copy(
        src_ref=h_hbm, dst_ref=h_buf.at[core], send_sem=h_sem.at[0], recv_sem=h_sem.at[1],
        device_id=(dp, tensor + 1 - 2 * core), device_id_type=MESH,
    )
    swap_h.start()
    load_v.wait()

    def backward(r, carry):
        queries = heads_to_rows(q_buf[r])
        grads = masked_grad(r)
        probs = p_buf[r]
        dprobs = contract(v_buf[r], grads, (1, 1))
        delta = jnp.sum(probs.astype(BF16).astype(F32) * dprobs, axis=0, keepdims=True)
        dscores = (probs * (dprobs - delta)).astype(BF16)
        dk_ref[r] = (contract(dscores, queries, (1, 0)) * factor).astype(BF16)
        dq = (contract(dscores, k_buf[r], (0, 0)) * factor).astype(BF16)
        for h in range(heads):
            dq_ref[r, :, h * HD : (h + 1) * HD] = dq[h * length : (h + 1) * length]
        return carry

    lax.fori_loop(0, rows, backward, 0)
    load_h.wait()
    swap_h.wait_recv()

    def gathered(s):
        @pl.when(core == 0)
        def _():
            for d in range(1, N):
                take_half(s, lax.rem(tensor + d, N)).wait_recv()

        @pl.when(core == 1)
        def _():
            for chip in range(chips):
                of = 2 * chip + s

                @pl.when(of != tensor)
                def _():
                    take_whole(of).wait_recv()

            parts = [gv_recv[2 * chip + s].astype(F32) for chip in range(chips)]
            for t in range(N):
                gv_chunk[s, t] = jnp.concatenate([x[8 * t : 8 * t + 8] for x in parts], axis=0).astype(BF16)

    def products(s, offsets):
        left = jnp.concatenate([gv_chunk[s, lax.rem(ring + d + N, N)] for d in offsets], axis=0)
        for k in range(2):
            both = contract(left, h_buf[k].reshape(tokens, cols), (1, 0))
            for i in range(len(offsets)):
                part[s, i, k] = both[i * piece : (i + 1) * piece]

    def hop(way, s, j):
        return pltpu.make_async_remote_copy(
            src_ref=r_send.at[way, s, j], dst_ref=r_recv.at[way, s, j],
            send_sem=rs_sem.at[way, s, j], recv_sem=rr_sem.at[way, s, j],
            device_id=(on_ring((1 if j else 2) * (1 - 2 * way)), tensor), device_id_type=MESH,
        )

    def first_sends(s):
        products(s, (3, -3, 4))
        r_send[s, s, 0] = part[s, 2].astype(BF16)
        hop(s, s, 0).start()
        for way in (s, 1 - s):
            r_send[way, s, 1] = part[s, way].astype(BF16)
            hop(way, s, 1).start()

    def pass_on(way, s, j):
        total = part[s, way]
        for k in ((0, 1) if j == 2 and way == s else (j - 1,)):
            hop(way, s, k).wait_recv()
            total = total + r_recv[way, s, k].astype(F32)
        r_send[way, s, j] = total.astype(BF16)
        hop(way, s, j).start()

    def second_sends(s):
        for way in (1 - s, s):
            pass_on(way, s, 2)
        products(s, (1, -1))

    def last_sends(s):
        for way in (1 - s, s):
            pass_on(way, s, 3)
        products(s, (0,))

    def place2(i):
        return i * (1 - core) + (2 * (i % 4) + i // 4) * core

    def cross(i):
        return pltpu.make_async_remote_copy(
            src_ref=s2_send.at[i], dst_ref=s2_recv.at[ring2],
            send_sem=s2s_sem.at[i], recv_sem=s2r_sem.at[ring2],
            device_id=(at_ring2(place2(i)), tensor), device_id_type=MESH,
        )

    def cross_in(of):
        return pltpu.make_async_remote_copy(
            src_ref=s2_send.at[0], dst_ref=s2_recv.at[of],
            send_sem=s2s_sem.at[0], recv_sem=s2r_sem.at[of],
            device_id=(at_ring2(of), tensor), device_id_type=MESH,
        )

    def if_away(i, act):
        @pl.when(place2(i) != ring2)
        def _():
            act(cross(i))

    def ring_end(s):
        total = part[s, 0]
        for way in (1 - s, s):
            hop(way, s, 3).wait_recv()
            total = total + r_recv[way, s, 3].astype(F32)
        total = total.reshape(2, 4, 8, cols)
        s2_send[4 * s : 4 * s + 4] = jnp.concatenate([total[0], total[1]], axis=1).astype(BF16)
        for i in range(4 * s, 4 * s + 4):
            if_away(i, lambda copy: copy.start())

    gathered(0)
    first_sends(0)
    gathered(1)
    first_sends(1)
    for s in range(2):
        products(s, (2, -2))
    second_sends(0)
    second_sends(1)
    last_sends(0)
    last_sends(1)
    ring_end(0)
    ring_end(1)

    for s in range(2):
        for chip in away:
            give_half(s, chip).wait_send()
        for way in range(2):
            for j in range(0 if way == s else 1, 4):
                hop(way, s, j).wait_send()
    for chip in away:
        give_whole(chip).wait_send()

    @pl.when(core == 0)
    def _():
        give_whole(own).wait_send()

    @pl.when(core == 1)
    def _():
        for s in range(2):
            give_half(s, own).wait_send()

    swap_h.wait_send()

    mine = ring2 * (1 - core) + (ring2 // 2 + 4 * lax.rem(ring2, 2)) * core
    total = s2_send[mine].astype(F32)
    for d in (1, 7, 2, 6, 3, 5, 4):
        of = lax.rem(ring2 + d, N)
        cross_in(of).wait_recv()
        total = total + s2_recv[of].astype(F32)
    for k in range(2):
        s3_send[k] = total[8 * k : 8 * k + 8]

    def finish(k):
        return pltpu.make_async_remote_copy(
            src_ref=s3_send.at[k], dst_ref=s3_recv.at[x_hi],
            send_sem=s3s_sem.at[k], recv_sem=s3r_sem.at[x_hi],
            device_id=(dp - x_hi + core, tensor - core + k), device_id_type=MESH,
        )

    def finish_in(of):
        return pltpu.make_async_remote_copy(
            src_ref=s3_send.at[0], dst_ref=s3_recv.at[of],
            send_sem=s3s_sem.at[0], recv_sem=s3r_sem.at[of],
            device_id=(far, tensor), device_id_type=MESH,
        )

    home = x_hi == core

    @pl.when(home)
    def _():
        finish(1 - core).start()

    @pl.when(jnp.logical_not(home))
    def _():
        for k in range(2):
            finish(k).start()

    for i in range(N):
        if_away(i, lambda copy: copy.wait_send())

    @pl.when(home)
    def _():
        finish_in(1 - x_hi).wait_recv()
        gw_ref[...] = s3_send[core] + s3_recv[1 - x_hi]
        finish(1 - core).wait_send()

    @pl.when(jnp.logical_not(home))
    def _():
        for of in range(2):
            finish_in(of).wait_recv()
        gw_ref[...] = s3_recv[0] + s3_recv[1]
        for k in range(2):
            finish(k).wait_send()


def local(queries, keys, values, hidden, grad_out, group_alive, positions):
    rows, length, model = queries.shape
    cols = hidden.shape[-1]
    heads = model // HD
    width = heads * length
    tokens = rows * length
    piece = HD // 4
    anywhere = pl.BlockSpec(memory_space=pl.ANY)
    inside = pl.BlockSpec(memory_space=pltpu.VMEM)
    dma = pltpu.SemaphoreType.DMA
    inputs = (queries, keys, values, hidden, grad_out, group_alive, positions)
    return pl.pallas_call(
        kernel,
        out_shape=(
            pltpu.VMEM(queries.shape, BF16),
            pltpu.VMEM(keys.shape, BF16),
            pltpu.VMEM((8, cols), F32),
        ),
        in_specs=[anywhere] * 7,
        out_specs=(inside,) * 3,
        scratch_shapes=[
            pltpu.VMEM(queries.shape, BF16),
            pltpu.VMEM(keys.shape, BF16),
            pltpu.VMEM(keys.shape, BF16),
            pltpu.VMEM(queries.shape, BF16),
            pltpu.VMEM((2,) + hidden.shape, BF16),
            pltpu.VMEM((length, width), jnp.int32),
            pltpu.VMEM((rows, length, width), F32),
            pltpu.VMEM((tokens, HD), F32),
            pltpu.SMEM(group_alive.shape, jnp.int32),
            pltpu.SMEM(positions.shape, jnp.int32),
            pltpu.VMEM((2, piece, tokens), BF16),
            pltpu.VMEM((2 * piece, tokens), BF16),
            pltpu.VMEM((N, 2 * piece, tokens), BF16),
            pltpu.VMEM((2, N, piece, tokens), BF16),
            pltpu.VMEM((2, 3, 2, piece, cols), F32),
            pltpu.VMEM((2, 2, 4, 2, piece, cols), BF16),
            pltpu.VMEM((2, 2, 4, 2, piece, cols), BF16),
            pltpu.VMEM((N, 16, cols), BF16),
            pltpu.VMEM((N, 16, cols), BF16),
            pltpu.VMEM((2, 8, cols), F32),
            pltpu.VMEM((2, 8, cols), F32),
            dma((2 * rows + 5,)),
            dma((2,)),
            dma((2, N // 2)),
            dma((2, N)),
            dma((N // 2,)),
            dma((N,)),
            dma((2, 2, 4)),
            dma((2, 2, 4)),
            dma((N,)),
            dma((N,)),
            dma((2,)),
            dma((2,)),
        ],
        compiler_params=pltpu.CompilerParams(
            collective_id=0, has_side_effects=True, vmem_limit_bytes=40 * 1024 * 1024
        ),
        cost_estimate=pl.CostEstimate(
            flops=10 * width * length * HD * rows + 2 * tokens * 1024 * cols,
            bytes_accessed=4000000,
            transcendentals=rows * width * length,
        ),
    )(*(pltpu.with_memory_space_constraint(x, pltpu.HBM) for x in inputs))


def solution(mesh):
    return jax.shard_map(
        local,
        mesh=mesh,
        in_specs=(
            P("dp", None, "tensor"),
            P("dp", None, "tensor"),
            P("dp", None, "tensor"),
            P("dp", None, "tensor"),
            P("dp", None, "tensor"),
            P(),
            P("dp", None),
        ),
        out_specs=(P("dp", None, "tensor"), P("dp", None, "tensor"), P("dp", "tensor")),
        check_vma=False,
    )
```
